32 devices in a mesh: grp: 2 (over x), row: 8 (over z, y), col: 2 (over core).
Axes of the slice: x: 2, y: 2, z: 4, core: 2. Of those that a mesh axis runs over, the one named last changes fastest.
Arguments:
- three_centre: bfloat16 [128, 1024, 1024], P(None, ('row', 'col')), may hold values from -6 to 6
- green_occ: bfloat16 [2048, 1024], P(('grp', 'row', 'col')), parts along dimension 0, may hold values from -0.25 to 0.25
- green_virt: bfloat16 [2048, 1024], P(('grp', 'row', 'col')), parts along dimension 0, may hold values from -0.25 to 0.25
- mask_three: int32 [1, 8, 8], replicated, may hold values 0 or 1
- mask_occ: int32 [16, 8], P('grp'), parts along dimension 0, may hold values 0 or 1
- mask_virt: int32 [16, 8], P('grp'), parts along dimension 0, may hold values 0 or 1
Outputs:
- half_done: bfloat16 [256, 1024, 1024], P('grp', ('row', 'col')), parts along dimension 0
- response: float32 [256, 128], P('grp'), parts along dimension 0
The draws below stay inside these ranges and needn't reach their ends.
There are 2 independent parts, one for each index of `grp`. The reference program is written for one: setup_inputs(seed, part) draws one part's arguments, and reference() takes and returns one part's arrays. A program takes and returns all parts, laid end to end along the dimension named above; an argument that names none is the same for every part. Nothing has to cross between parts.
All inputs are finite; a program needn't handle non-finite values.
Results may differ from the reference program's by a relative error of at most 0.0053.
Values may be sent and summed in bfloat16 or wider, within the bound.
A program may use at most 192 MiB of HBM per device.

```python
import jax
import jax.numpy as jnp
from jax import lax

BLK = 128
NAO = 1024
NP = 128
NB = 8
NPB = 1


def with_ends(array, key, smallest, largest):
    extent = array.shape
    spot = [jax.random.randint(jax.random.fold_in(key, axis), (), 0, extent[axis]) for axis in range(len(extent))]
    array = array.at[tuple(spot)].set(smallest)
    longest = extent.index(max(extent))
    spot[longest] = (spot[longest] + 1) % extent[longest]
    return array.at[tuple(spot)].set(largest)


def block_scale(rng, shape, shards, low, top_value):
    level = 1.0
    for position, blocks in shards:
        draws = jax.random.uniform(jax.random.fold_in(jax.random.fold_in(rng, 6), position), (blocks,), jnp.float32, low / len(shards), top_value / len(shards))
        level = level * jnp.repeat(jnp.exp(draws), shape[position] // blocks).reshape((-1,) + (1,) * (len(shape) - 1 - position))
    return level


def centred(key, dims, width, bound, shards=(), kind=jnp.bfloat16):
    loudness = block_scale(key, dims, shards, -0.22, 0.18) if shards else 1.0
    values = jax.random.normal(key, dims, jnp.float32) * width * loudness
    return jnp.minimum(jnp.maximum(values, -bound), bound).astype(kind)


def setup_inputs(seed: int = 0, part: int = 0) -> dict:
    key_list = jax.random.split(jax.random.key(seed), 7)
    part_splits = jax.random.split(jax.random.fold_in(key_list[6], part), 7)
    three_centre = centred(key_list[0], (NP, NAO, NAO), 1.0, 6.0, ((1, 16),))
    green_occ = centred(part_splits[1], (NAO, NAO), (NAO // 2) ** -0.5, 0.25, ((0, 16),))
    green_virt = centred(part_splits[2], (NAO, NAO), (NAO // 2) ** -0.5, 0.25, ((0, 16),))
    mask_three = with_ends((jax.random.randint(key_list[3], (NPB, NB, NB), 0, 2) < 1).astype(jnp.int32), jax.random.fold_in(key_list[3], 1), 0, 1)
    mask_occ = with_ends((jax.random.randint(part_splits[4], (NB, NB), 0, 2) < 1).astype(jnp.int32), jax.random.fold_in(part_splits[4], 1), 0, 1)
    mask_virt = with_ends((jax.random.randint(part_splits[5], (NB, NB), 0, 2) < 1).astype(jnp.int32), jax.random.fold_in(part_splits[5], 1), 0, 1)
    return {"three_centre": three_centre, "green_occ": green_occ, "green_virt": green_virt, "mask_three": mask_three, "mask_occ": mask_occ, "mask_virt": mask_virt}


def expand_full(small_mask):
    return jnp.repeat(jnp.repeat(small_mask, BLK, axis=0), BLK, axis=1)


def reference(three_centre, green_occ, green_virt, mask_three, mask_occ, mask_virt):
    occ_masked = green_occ * expand_full(mask_occ).astype(jnp.bfloat16)
    virt_masked = green_virt * expand_full(mask_virt).astype(jnp.bfloat16)
    ri_blocks = NP // BLK
    block_count = NAO // BLK
    masked = (three_centre.reshape(ri_blocks, BLK, block_count, BLK, block_count, BLK)
              * mask_three[:, None, :, None, :, None].astype(jnp.bfloat16)).reshape(NP, NAO, NAO)
    masked_flat = masked.reshape(NP, NAO * NAO)

    def one_block(slab):
        transformed = jnp.dot(slab.reshape(BLK * NAO, NAO), occ_masked,
                              preferred_element_type=jnp.float32).astype(jnp.bfloat16)
        swapped = jnp.swapaxes(transformed.reshape(BLK, NAO, NAO), 1, 2)
        xform = jnp.dot(swapped.reshape(BLK * NAO, NAO), virt_masked,
                        preferred_element_type=jnp.float32).astype(jnp.bfloat16)
        block_response = jnp.dot(xform.reshape(BLK, NAO * NAO), masked_flat.T,
                                 preferred_element_type=jnp.float32)
        return swapped, block_response

    swapped, parts = lax.map(one_block, masked.reshape(ri_blocks, BLK, NAO, NAO))
    response = -parts.reshape(NP, NP) / NAO
    return swapped.reshape(NP, NAO, NAO), response
```

```python
import functools

import jax
import jax.numpy as jnp
from jax import lax
from jax.experimental import pallas as pl
from jax.experimental.pallas import tpu as pltpu
from jax.sharding import PartitionSpec as P

AXES = ("row", "col")
CHUNKS = 4
STEP = 8
VMEM = 48 * 2**20


def expand_rows(small_mask, first_row, row_count, block_size):
    tall = jnp.repeat(small_mask, block_size, axis=0)
    tall = lax.dynamic_slice_in_dim(tall, first_row, row_count, 0)
    return jnp.repeat(tall, block_size, axis=1)


def local_plain(three_centre, green_occ, green_virt, mask_three, mask_occ, mask_virt):
    dev_index = lax.axis_index(("row", "col"))
    ri_count, local_rows, ao_count = three_centre.shape
    block_count = mask_occ.shape[0]
    block_size = ao_count // block_count
    ri_blocks = mask_three.shape[0]
    first_row = dev_index * local_rows
    occ_local = green_occ * expand_rows(mask_occ, first_row, local_rows, block_size).astype(
        jnp.bfloat16
    )
    virt_local = green_virt * expand_rows(mask_virt, first_row, local_rows, block_size).astype(
        jnp.bfloat16
    )
    three_mask = lax.dynamic_slice_in_dim(
        jnp.repeat(mask_three, block_size, axis=1), first_row, local_rows, 1
    )
    masked = (
        three_centre.reshape(ri_blocks, block_size, local_rows, block_count, block_size)
        * three_mask[:, None, :, :, None].astype(jnp.bfloat16)
    ).reshape(ri_count, local_rows, ao_count)
    masked_rows = masked.reshape(ri_count * local_rows, ao_count)
    occ_full, virt_full = (
        lax.all_gather(occ_local, ("row", "col"), axis=0, tiled=True),
        lax.all_gather(virt_local, ("row", "col"), axis=0, tiled=True),
    )
    first_sum = jnp.dot(masked_rows, occ_full, preferred_element_type=jnp.float32)
    transformed = first_sum.astype(jnp.bfloat16).reshape(ri_count, local_rows, ao_count)
    arrived = lax.all_to_all(transformed, ("row", "col"), split_axis=2, concat_axis=1, tiled=True)
    swapped = jnp.swapaxes(arrived, 1, 2)
    swapped_rows = swapped.reshape(ri_count * local_rows, ao_count)
    second_sum = jnp.dot(swapped_rows, virt_full, preferred_element_type=jnp.float32)
    xform = second_sum.astype(jnp.bfloat16).reshape(ri_count, local_rows * ao_count)
    partial_value = lax.dot_general(
        xform,
        masked.reshape(ri_count, local_rows * ao_count),
        (((1,), (1,)), ((), ())),
        preferred_element_type=jnp.float32,
    )
    summed = lax.psum(partial_value, ("row", "col"))
    response = -summed / ao_count
    return (swapped, response)


def first_kernel(weight_ref, rows_ref, sent_ref):
    step, rows, depth = rows_ref.shape
    flat = rows_ref[...].reshape(step * rows, depth)
    product = lax.dot_general(
        weight_ref[...], flat, (((1,), (1,)), ((), ())), preferred_element_type=jnp.float32
    ).astype(jnp.bfloat16)
    owners, pairs, width, lanes = sent_ref.shape
    for pair in range(pairs):
        sent_ref[:, pair] = product[:, pair * lanes : (pair + 1) * lanes].reshape(
            owners, width, lanes
        )


def second_kernel(came_ref, weight_ref, *refs):
    half_ref, xform_ref = refs[-2:]
    owners, pairs, width, lanes = came_ref.shape
    for pair in range(pairs):
        for tile in range(owners // 2):
            even, odd = came_ref[2 * tile, pair], came_ref[2 * tile + 1, pair]
            spot = slice(tile * lanes, (tile + 1) * lanes)
            half_ref[2 * pair, :, spot] = jnp.concatenate(
                [even[:, :width], odd[:, :width]], axis=-1
            )
            half_ref[2 * pair + 1, :, spot] = jnp.concatenate(
                [even[:, width:], odd[:, width:]], axis=-1
            )
    step, rows, depth = half_ref.shape
    product = jnp.dot(
        half_ref[...].reshape(step * rows, depth),
        weight_ref[...],
        preferred_element_type=jnp.float32,
    )
    xform_ref[...] = product.astype(jnp.bfloat16).reshape(step, rows, depth)


def transform_chunk(weight, three_centre, chunk, chunk_size, owners):
    ri_count, rows, depth = three_centre.shape
    steps = chunk_size // STEP
    return pl.pallas_call(
        first_kernel,
        grid=(steps,),
        in_specs=[
            pl.BlockSpec((depth, depth), lambda i: (0, 0)),
            pl.BlockSpec((STEP, rows, depth), lambda i: (chunk * steps + i, 0, 0)),
        ],
        out_specs=pl.BlockSpec((owners, STEP // 2, rows, 2 * rows), lambda i: (0, i, 0, 0)),
        out_shape=jax.ShapeDtypeStruct((owners, chunk_size // 2, rows, 2 * rows), jnp.bfloat16),
        compiler_params=pltpu.CompilerParams(vmem_limit_bytes=VMEM),
        cost_estimate=pl.CostEstimate(
            flops=2 * chunk_size * rows * depth * depth,
            bytes_accessed=4 * chunk_size * rows * depth + 2 * depth * depth,
            transcendentals=0,
        ),
    )(weight, three_centre)


def finish_chunk(came, weight, half, chunk, chunk_size, ri_count):
    owners, pairs, rows, lanes = came.shape
    depth = weight.shape[0]
    steps = chunk_size // STEP
    operands = [came, weight]
    in_specs = [
        pl.BlockSpec((owners, STEP // 2, rows, lanes), lambda i: (0, i, 0, 0)),
        pl.BlockSpec((depth, depth), lambda i: (0, 0)),
    ]
    aliases = {}
    if half is not None:
        operands.append(half)
        in_specs.append(pl.BlockSpec(memory_space=pl.ANY))
        aliases = {2: 0}
    return pl.pallas_call(
        second_kernel,
        grid=(steps,),
        in_specs=in_specs,
        out_specs=[
            pl.BlockSpec((STEP, rows, depth), lambda i: (chunk * steps + i, 0, 0)),
            pl.BlockSpec((STEP, rows, depth), lambda i: (i, 0, 0)),
        ],
        out_shape=[
            jax.ShapeDtypeStruct((ri_count, rows, depth), jnp.bfloat16),
            jax.ShapeDtypeStruct((chunk_size, rows, depth), jnp.bfloat16),
        ],
        input_output_aliases=aliases,
        compiler_params=pltpu.CompilerParams(vmem_limit_bytes=VMEM),
        cost_estimate=pl.CostEstimate(
            flops=2 * chunk_size * rows * depth * depth,
            bytes_accessed=6 * chunk_size * rows * depth + 2 * depth * depth,
            transcendentals=0,
        ),
    )(*operands)


def spread(mask, block_size):
    return jnp.repeat(jnp.repeat(mask, block_size, 0), block_size, 1).astype(jnp.bfloat16)


def sum_over_devices(value, owners):
    pieces = value.reshape(owners, value.shape[0] // owners, value.shape[1])
    pieces = lax.all_to_all(pieces, AXES, split_axis=0, concat_axis=0, tiled=True)
    total = jnp.sum(pieces, axis=0)
    copies = jnp.broadcast_to(total[None], pieces.shape)
    copies = lax.all_to_all(copies, AXES, split_axis=0, concat_axis=0, tiled=True)
    return copies.reshape(value.shape)


def local_fused(owners, three_centre, green_occ, green_virt, mask_three, mask_occ, mask_virt):
    ri_count, rows, depth = three_centre.shape
    block_size = depth // mask_occ.shape[0]
    chunk_size = ri_count // CHUNKS
    own_block = lax.axis_index(AXES) * rows // block_size
    own_mask = lax.dynamic_slice_in_dim(mask_three[0], own_block, 1, 0)
    occ_full = lax.all_gather(green_occ, AXES, axis=0, tiled=True)
    virt_full = lax.all_gather(green_virt, AXES, axis=0, tiled=True)
    occ_weight = occ_full.T * spread(mask_occ.T * own_mask, block_size)
    virt_weight = virt_full * spread(mask_virt * own_mask, block_size)
    sent = [
        transform_chunk(occ_weight, three_centre, chunk, chunk_size, owners)
        for chunk in range(CHUNKS)
    ]
    came = [
        lax.all_to_all(block, AXES, split_axis=0, concat_axis=0, tiled=True) for block in sent
    ]
    half, parts = None, []
    for chunk in range(CHUNKS):
        half, xform = finish_chunk(came[chunk], virt_weight, half, chunk, chunk_size, ri_count)
        parts.append(
            lax.dot_general(
                xform,
                three_centre,
                (((1, 2), (1, 2)), ((), ())),
                preferred_element_type=jnp.float32,
            )
        )
    response = -sum_over_devices(jnp.concatenate(parts, axis=0), owners) / depth
    return half, response


def local(owners, three_centre, green_occ, green_virt, mask_three, mask_occ, mask_virt):
    ri_count, rows, depth = three_centre.shape
    block_size = depth // mask_occ.shape[0]
    fits = (
        mask_three.shape[0] == 1
        and 2 * rows == 128
        and block_size % rows == 0
        and owners % 2 == 0
        and owners * rows == depth
        and ri_count % (CHUNKS * STEP) == 0
        and ri_count % owners == 0
    )
    body = functools.partial(local_fused, owners) if fits else local_plain
    return body(three_centre, green_occ, green_virt, mask_three, mask_occ, mask_virt)


def solution(mesh):
    owners = mesh.shape["row"] * mesh.shape["col"]
    in_specs = (
        P(None, ("row", "col"), None),
        P(("grp", "row", "col"), None),
        P(("grp", "row", "col"), None),
        P(),
        P("grp", None),
        P("grp", None),
    )
    out_specs = (P("grp", ("row", "col"), None), P("grp", None))
    return jax.shard_map(
        functools.partial(local, owners), mesh=mesh, in_specs=in_specs, out_specs=out_specs, check_vma=False)
```

```python
import functools

import jax
import jax.numpy as jnp
from jax import lax
from jax.experimental import pallas as pl
from jax.experimental.pallas import tpu as pltpu
from jax.sharding import PartitionSpec as P

AXES = ("row", "col")
SHARES = (1, 3, 3, 1)
STEP = 8
VMEM = 48 * 2**20


def expand_rows(small_mask, first_row, row_count, block_size):
    tall = jnp.repeat(small_mask, block_size, axis=0)
    tall = lax.dynamic_slice_in_dim(tall, first_row, row_count, 0)
    return jnp.repeat(tall, block_size, axis=1)


def local_plain(three_centre, green_occ, green_virt, mask_three, mask_occ, mask_virt):
    dev_index = lax.axis_index(("row", "col"))
    ri_count, local_rows, ao_count = three_centre.shape
    block_count = mask_occ.shape[0]
    block_size = ao_count // block_count
    ri_blocks = mask_three.shape[0]
    first_row = dev_index * local_rows
    occ_local = green_occ * expand_rows(mask_occ, first_row, local_rows, block_size).astype(
        jnp.bfloat16
    )
    virt_local = green_virt * expand_rows(mask_virt, first_row, local_rows, block_size).astype(
        jnp.bfloat16
    )
    three_mask = lax.dynamic_slice_in_dim(
        jnp.repeat(mask_three, block_size, axis=1), first_row, local_rows, 1
    )
    masked = (
        three_centre.reshape(ri_blocks, block_size, local_rows, block_count, block_size)
        * three_mask[:, None, :, :, None].astype(jnp.bfloat16)
    ).reshape(ri_count, local_rows, ao_count)
    masked_rows = masked.reshape(ri_count * local_rows, ao_count)
    occ_full, virt_full = (
        lax.all_gather(occ_local, ("row", "col"), axis=0, tiled=True),
        lax.all_gather(virt_local, ("row", "col"), axis=0, tiled=True),
    )
    first_sum = jnp.dot(masked_rows, occ_full, preferred_element_type=jnp.float32)
    transformed = first_sum.astype(jnp.bfloat16).reshape(ri_count, local_rows, ao_count)
    arrived = lax.all_to_all(transformed, ("row", "col"), split_axis=2, concat_axis=1, tiled=True)
    swapped = jnp.swapaxes(arrived, 1, 2)
    swapped_rows = swapped.reshape(ri_count * local_rows, ao_count)
    second_sum = jnp.dot(swapped_rows, virt_full, preferred_element_type=jnp.float32)
    xform = second_sum.astype(jnp.bfloat16).reshape(ri_count, local_rows * ao_count)
    partial_value = lax.dot_general(
        xform,
        masked.reshape(ri_count, local_rows * ao_count),
        (((1,), (1,)), ((), ())),
        preferred_element_type=jnp.float32,
    )
    summed = lax.psum(partial_value, ("row", "col"))
    response = -summed / ao_count
    return (swapped, response)


def first_kernel(weight_ref, rows_ref, sent_ref):
    step, rows, depth = rows_ref.shape
    flat = rows_ref[...].reshape(step * rows, depth)
    product = lax.dot_general(
        weight_ref[...], flat, (((1,), (1,)), ((), ())), preferred_element_type=jnp.float32
    ).astype(jnp.bfloat16)
    owners, pairs, width, lanes = sent_ref.shape
    for pair in range(pairs):
        sent_ref[:, pair] = product[:, pair * lanes : (pair + 1) * lanes].reshape(
            owners, width, lanes
        )


def second_kernel(came_ref, weight_ref, *refs):
    half_ref, xform_ref = refs[-2:]
    owners, pairs, width, lanes = came_ref.shape
    for pair in range(pairs):
        for tile in range(owners // 2):
            even, odd = came_ref[2 * tile, pair], came_ref[2 * tile + 1, pair]
            spot = slice(tile * lanes, (tile + 1) * lanes)
            half_ref[2 * pair, :, spot] = jnp.concatenate(
                [even[:, :width], odd[:, :width]], axis=-1
            )
            half_ref[2 * pair + 1, :, spot] = jnp.concatenate(
                [even[:, width:], odd[:, width:]], axis=-1
            )
    step, rows, depth = half_ref.shape
    product = jnp.dot(
        half_ref[...].reshape(step * rows, depth),
        weight_ref[...],
        preferred_element_type=jnp.float32,
    )
    xform_ref[...] = product.astype(jnp.bfloat16).reshape(step, rows, depth)


def transform_chunk(weight, three_centre, first, chunk_size, owners):
    ri_count, rows, depth = three_centre.shape
    steps, offset = chunk_size // STEP, first // STEP
    return pl.pallas_call(
        first_kernel,
        grid=(steps,),
        in_specs=[
            pl.BlockSpec((depth, depth), lambda i: (0, 0)),
            pl.BlockSpec((STEP, rows, depth), lambda i: (offset + i, 0, 0)),
        ],
        out_specs=pl.BlockSpec((owners, STEP // 2, rows, 2 * rows), lambda i: (0, i, 0, 0)),
        out_shape=jax.ShapeDtypeStruct((owners, chunk_size // 2, rows, 2 * rows), jnp.bfloat16),
        compiler_params=pltpu.CompilerParams(vmem_limit_bytes=VMEM),
        cost_estimate=pl.CostEstimate(
            flops=2 * chunk_size * rows * depth * depth,
            bytes_accessed=4 * chunk_size * rows * depth + 2 * depth * depth,
            transcendentals=0,
        ),
    )(weight, three_centre)


def finish_chunk(came, weight, half, first, chunk_size, ri_count):
    owners, pairs, rows, lanes = came.shape
    depth = weight.shape[0]
    steps, offset = chunk_size // STEP, first // STEP
    operands = [came, weight]
    in_specs = [
        pl.BlockSpec((owners, STEP // 2, rows, lanes), lambda i: (0, i, 0, 0)),
        pl.BlockSpec((depth, depth), lambda i: (0, 0)),
    ]
    aliases = {}
    if half is not None:
        operands.append(half)
        in_specs.append(pl.BlockSpec(memory_space=pl.ANY))
        aliases = {2: 0}
    return pl.pallas_call(
        second_kernel,
        grid=(steps,),
        in_specs=in_specs,
        out_specs=[
            pl.BlockSpec((STEP, rows, depth), lambda i: (offset + i, 0, 0)),
            pl.BlockSpec((STEP, rows, depth), lambda i: (i, 0, 0)),
        ],
        out_shape=[
            jax.ShapeDtypeStruct((ri_count, rows, depth), jnp.bfloat16),
            jax.ShapeDtypeStruct((chunk_size, rows, depth), jnp.bfloat16),
        ],
        input_output_aliases=aliases,
        compiler_params=pltpu.CompilerParams(vmem_limit_bytes=VMEM),
        cost_estimate=pl.CostEstimate(
            flops=2 * chunk_size * rows * depth * depth,
            bytes_accessed=6 * chunk_size * rows * depth + 2 * depth * depth,
            transcendentals=0,
        ),
    )(*operands)


def spread(mask, block_size):
    return jnp.repeat(jnp.repeat(mask, block_size, 0), block_size, 1).astype(jnp.bfloat16)


def sum_over_devices(value, owners):
    pieces = value.reshape(owners, value.shape[0] // owners, value.shape[1])
    pieces = lax.all_to_all(pieces, AXES, split_axis=0, concat_axis=0, tiled=True)
    total = jnp.sum(pieces, axis=0)
    copies = jnp.broadcast_to(total[None], pieces.shape)
    copies = lax.all_to_all(copies, AXES, split_axis=0, concat_axis=0, tiled=True)
    return copies.reshape(value.shape)


def local_fused(owners, three_centre, green_occ, green_virt, mask_three, mask_occ, mask_virt):
    ri_count, rows, depth = three_centre.shape
    block_size = depth // mask_occ.shape[0]
    sizes = [ri_count // sum(SHARES) * share for share in SHARES]
    firsts = [sum(sizes[:chunk]) for chunk in range(len(sizes))]
    own_block = lax.axis_index(AXES) * rows // block_size
    own_mask = lax.dynamic_slice_in_dim(mask_three[0], own_block, 1, 0)
    both = jnp.concatenate([green_occ, green_virt], axis=1)
    both = lax.all_gather(both, AXES, axis=0, tiled=True)
    occ_full, virt_full = both[:, :depth], both[:, depth:]
    occ_weight = occ_full.T * spread(mask_occ.T * own_mask, block_size)
    virt_weight = virt_full * spread(mask_virt * own_mask, block_size)
    three_flat = lax.optimization_barrier(three_centre.reshape(ri_count, rows * depth))
    half, parts = None, []
    came = {}

    def send(chunk):
        block = transform_chunk(occ_weight, three_centre, firsts[chunk], sizes[chunk], owners)
        if chunk >= 2:
            block, came[chunk - 1], parts[chunk - 2] = lax.optimization_barrier(
                (block, came[chunk - 1], parts[chunk - 2])
            )
        elif chunk == 1:
            block, came[0] = lax.optimization_barrier((block, came[0]))
        came[chunk] = lax.all_to_all(block, AXES, split_axis=0, concat_axis=0, tiled=True)

    send(0)
    for chunk in range(len(sizes)):
        if chunk + 1 < len(sizes):
            send(chunk + 1)
        half, xform = finish_chunk(
            came[chunk], virt_weight, half, firsts[chunk], sizes[chunk], ri_count
        )
        flat = lax.optimization_barrier(xform.reshape(sizes[chunk], rows * depth))
        parts.append(
            lax.dot_general(
                flat, three_flat, (((1,), (1,)), ((), ())), preferred_element_type=jnp.float32
            )
        )
    response = -sum_over_devices(jnp.concatenate(parts, axis=0), owners) / depth
    return half, response


def local(owners, three_centre, green_occ, green_virt, mask_three, mask_occ, mask_virt):
    ri_count, rows, depth = three_centre.shape
    block_size = depth // mask_occ.shape[0]
    fits = (
        mask_three.shape[0] == 1
        and 2 * rows == 128
        and block_size % rows == 0
        and owners % 2 == 0
        and owners * rows == depth
        and ri_count % (sum(SHARES) * STEP) == 0
        and ri_count % owners == 0
    )
    body = functools.partial(local_fused, owners) if fits else local_plain
    return body(three_centre, green_occ, green_virt, mask_three, mask_occ, mask_virt)


def solution(mesh):
    owners = mesh.shape["row"] * mesh.shape["col"]
    in_specs = (
        P(None, ("row", "col"), None),
        P(("grp", "row", "col"), None),
        P(("grp", "row", "col"), None),
        P(),
        P("grp", None),
        P("grp", None),
    )
    out_specs = (P("grp", ("row", "col"), None), P("grp", None))
    return jax.shard_map(
        functools.partial(local, owners), mesh=mesh, in_specs=in_specs, out_specs=out_specs, check_vma=False)
```

```python
import functools

import jax
import jax.numpy as jnp
from jax import lax
from jax.experimental import pallas as pl
from jax.experimental.pallas import tpu as pltpu
from jax.sharding import PartitionSpec as P

AXES = ("row", "col")
SHARES = (1, 3, 3, 1)
STEP = 8
VMEM = 48 * 2**20


def expand_rows(small_mask, first_row, row_count, block_size):
    tall = jnp.repeat(small_mask, block_size, axis=0)
    tall = lax.dynamic_slice_in_dim(tall, first_row, row_count, 0)
    return jnp.repeat(tall, block_size, axis=1)


def local_plain(three_centre, green_occ, green_virt, mask_three, mask_occ, mask_virt):
    dev_index = lax.axis_index(("row", "col"))
    ri_count, local_rows, ao_count = three_centre.shape
    block_count = mask_occ.shape[0]
    block_size = ao_count // block_count
    ri_blocks = mask_three.shape[0]
    first_row = dev_index * local_rows
    occ_local = green_occ * expand_rows(mask_occ, first_row, local_rows, block_size).astype(
        jnp.bfloat16
    )
    virt_local = green_virt * expand_rows(mask_virt, first_row, local_rows, block_size).astype(
        jnp.bfloat16
    )
    three_mask = lax.dynamic_slice_in_dim(
        jnp.repeat(mask_three, block_size, axis=1), first_row, local_rows, 1
    )
    masked = (
        three_centre.reshape(ri_blocks, block_size, local_rows, block_count, block_size)
        * three_mask[:, None, :, :, None].astype(jnp.bfloat16)
    ).reshape(ri_count, local_rows, ao_count)
    masked_rows = masked.reshape(ri_count * local_rows, ao_count)
    occ_full, virt_full = (
        lax.all_gather(occ_local, ("row", "col"), axis=0, tiled=True),
        lax.all_gather(virt_local, ("row", "col"), axis=0, tiled=True),
    )
    first_sum = jnp.dot(masked_rows, occ_full, preferred_element_type=jnp.float32)
    transformed = first_sum.astype(jnp.bfloat16).reshape(ri_count, local_rows, ao_count)
    arrived = lax.all_to_all(transformed, ("row", "col"), split_axis=2, concat_axis=1, tiled=True)
    swapped = jnp.swapaxes(arrived, 1, 2)
    swapped_rows = swapped.reshape(ri_count * local_rows, ao_count)
    second_sum = jnp.dot(swapped_rows, virt_full, preferred_element_type=jnp.float32)
    xform = second_sum.astype(jnp.bfloat16).reshape(ri_count, local_rows * ao_count)
    partial_value = lax.dot_general(
        xform,
        masked.reshape(ri_count, local_rows * ao_count),
        (((1,), (1,)), ((), ())),
        preferred_element_type=jnp.float32,
    )
    summed = lax.psum(partial_value, ("row", "col"))
    response = -summed / ao_count
    return (swapped, response)


def first_kernel(weight_ref, rows_ref, sent_ref):
    step, rows, depth = rows_ref.shape
    flat = rows_ref[...].reshape(step * rows, depth)
    product = lax.dot_general(
        weight_ref[...], flat, (((1,), (1,)), ((), ())), preferred_element_type=jnp.float32
    ).astype(jnp.bfloat16)
    owners, pairs, width, lanes = sent_ref.shape
    for pair in range(pairs):
        sent_ref[:, pair] = product[:, pair * lanes : (pair + 1) * lanes].reshape(
            owners, width, lanes
        )


def second_kernel(came_ref, weight_ref, *refs):
    half_ref, xform_ref = refs[-2:]
    owners, pairs, width, lanes = came_ref.shape
    for pair in range(pairs):
        for tile in range(owners // 2):
            even, odd = came_ref[2 * tile, pair], came_ref[2 * tile + 1, pair]
            spot = slice(tile * lanes, (tile + 1) * lanes)
            half_ref[2 * pair, :, spot] = jnp.concatenate(
                [even[:, :width], odd[:, :width]], axis=-1
            )
            half_ref[2 * pair + 1, :, spot] = jnp.concatenate(
                [even[:, width:], odd[:, width:]], axis=-1
            )
    step, rows, depth = half_ref.shape
    product = jnp.dot(
        half_ref[...].reshape(step * rows, depth),
        weight_ref[...],
        preferred_element_type=jnp.float32,
    )
    xform_ref[...] = product.astype(jnp.bfloat16).reshape(step, rows, depth)


def transform_chunk(weight, three_centre, first, chunk_size, owners):
    ri_count, rows, depth = three_centre.shape
    steps, offset = chunk_size // STEP, first // STEP
    return pl.pallas_call(
        first_kernel,
        grid=(steps,),
        in_specs=[
            pl.BlockSpec((depth, depth), lambda i: (0, 0)),
            pl.BlockSpec((STEP, rows, depth), lambda i: (offset + i, 0, 0)),
        ],
        out_specs=pl.BlockSpec((owners, STEP // 2, rows, 2 * rows), lambda i: (0, i, 0, 0)),
        out_shape=jax.ShapeDtypeStruct((owners, chunk_size // 2, rows, 2 * rows), jnp.bfloat16),
        compiler_params=pltpu.CompilerParams(vmem_limit_bytes=VMEM),
        cost_estimate=pl.CostEstimate(
            flops=2 * chunk_size * rows * depth * depth,
            bytes_accessed=4 * chunk_size * rows * depth + 2 * depth * depth,
            transcendentals=0,
        ),
    )(weight, three_centre)


def finish_chunk(came, weight, half, first, chunk_size, ri_count):
    owners, pairs, rows, lanes = came.shape
    depth = weight.shape[0]
    steps, offset = chunk_size // STEP, first // STEP
    operands = [came, weight]
    in_specs = [
        pl.BlockSpec((owners, STEP // 2, rows, lanes), lambda i: (0, i, 0, 0)),
        pl.BlockSpec((depth, depth), lambda i: (0, 0)),
    ]
    aliases = {}
    if half is not None:
        operands.append(half)
        in_specs.append(pl.BlockSpec(memory_space=pl.ANY))
        aliases = {2: 0}
    return pl.pallas_call(
        second_kernel,
        grid=(steps,),
        in_specs=in_specs,
        out_specs=[
            pl.BlockSpec((STEP, rows, depth), lambda i: (offset + i, 0, 0)),
            pl.BlockSpec((STEP, rows, depth), lambda i: (i, 0, 0)),
        ],
        out_shape=[
            jax.ShapeDtypeStruct((ri_count, rows, depth), jnp.bfloat16),
            jax.ShapeDtypeStruct((chunk_size, rows, depth), jnp.bfloat16),
        ],
        input_output_aliases=aliases,
        compiler_params=pltpu.CompilerParams(vmem_limit_bytes=VMEM),
        cost_estimate=pl.CostEstimate(
            flops=2 * chunk_size * rows * depth * depth,
            bytes_accessed=6 * chunk_size * rows * depth + 2 * depth * depth,
            transcendentals=0,
        ),
    )(*operands)


def spread(mask, block_size):
    return jnp.repeat(jnp.repeat(mask, block_size, 0), block_size, 1).astype(jnp.bfloat16)


def sum_over_devices(value, owners):
    pieces = value.reshape(owners, value.shape[0] // owners, value.shape[1])
    pieces = lax.all_to_all(pieces, AXES, split_axis=0, concat_axis=0, tiled=True)
    total = jnp.sum(pieces, axis=0)
    copies = jnp.broadcast_to(total[None], pieces.shape)
    copies = lax.all_to_all(copies, AXES, split_axis=0, concat_axis=0, tiled=True)
    return copies.reshape(value.shape)


def local_fused(owners, three_centre, green_occ, green_virt, mask_three, mask_occ, mask_virt):
    ri_count, rows, depth = three_centre.shape
    block_size = depth // mask_occ.shape[0]
    sizes = [ri_count // sum(SHARES) * share for share in SHARES]
    firsts = [sum(sizes[:chunk]) for chunk in range(len(sizes))]
    own_block = lax.axis_index(AXES) * rows // block_size
    own_mask = lax.dynamic_slice_in_dim(mask_three[0], own_block, 1, 0)
    occ_full = lax.all_gather(green_occ, AXES, axis=0, tiled=True)
    virt_full = lax.all_gather(green_virt, AXES, axis=0, tiled=True)
    occ_weight = occ_full.T * spread(mask_occ.T * own_mask, block_size)
    virt_weight = virt_full * spread(mask_virt * own_mask, block_size)
    three_flat = lax.optimization_barrier(three_centre.reshape(ri_count, rows * depth))
    half, parts = None, []
    came = {}

    def send(chunk):
        block = transform_chunk(occ_weight, three_centre, firsts[chunk], sizes[chunk], owners)
        if chunk >= 2:
            block, came[chunk - 1], parts[chunk - 2] = lax.optimization_barrier(
                (block, came[chunk - 1], parts[chunk - 2])
            )
        elif chunk == 1:
            block, came[0] = lax.optimization_barrier((block, came[0]))
        came[chunk] = lax.all_to_all(block, AXES, split_axis=0, concat_axis=0, tiled=True)

    send(0)
    for chunk in range(len(sizes)):
        if chunk + 1 < len(sizes):
            send(chunk + 1)
        half, xform = finish_chunk(
            came[chunk], virt_weight, half, firsts[chunk], sizes[chunk], ri_count
        )
        flat = lax.optimization_barrier(xform.reshape(sizes[chunk], rows * depth))
        parts.append(
            lax.dot_general(
                flat, three_flat, (((1,), (1,)), ((), ())), preferred_element_type=jnp.float32
            )
        )
    response = -sum_over_devices(jnp.concatenate(parts, axis=0), owners) / depth
    return half, response


def local(owners, three_centre, green_occ, green_virt, mask_three, mask_occ, mask_virt):
    ri_count, rows, depth = three_centre.shape
    block_size = depth // mask_occ.shape[0]
    fits = (
        mask_three.shape[0] == 1
        and 2 * rows == 128
        and block_size % rows == 0
        and owners % 2 == 0
        and owners * rows == depth
        and ri_count % (sum(SHARES) * STEP) == 0
        and ri_count % owners == 0
    )
    body = functools.partial(local_fused, owners) if fits else local_plain
    return body(three_centre, green_occ, green_virt, mask_three, mask_occ, mask_virt)


def solution(mesh):
    owners = mesh.shape["row"] * mesh.shape["col"]
    in_specs = (
        P(None, ("row", "col"), None),
        P(("grp", "row", "col"), None),
        P(("grp", "row", "col"), None),
        P(),
        P("grp", None),
        P("grp", None),
    )
    out_specs = (P("grp", ("row", "col"), None), P("grp", None))
    return jax.shard_map(
        functools.partial(local, owners), mesh=mesh, in_specs=in_specs, out_specs=out_specs, check_vma=False)
```

```python
import functools

import jax
import jax.numpy as jnp
from jax import lax
from jax.experimental import pallas as pl
from jax.experimental.pallas import tpu as pltpu
from jax.sharding import PartitionSpec as P

AXES = ("row", "col")
SHARES = (2, 11, 3)
STEP = 8
VMEM = 48 * 2**20


def expand_rows(small_mask, first_row, row_count, block_size):
    tall = jnp.repeat(small_mask, block_size, axis=0)
    tall = lax.dynamic_slice_in_dim(tall, first_row, row_count, 0)
    return jnp.repeat(tall, block_size, axis=1)


def local_plain(three_centre, green_occ, green_virt, mask_three, mask_occ, mask_virt):
    dev_index = lax.axis_index(("row", "col"))
    ri_count, local_rows, ao_count = three_centre.shape
    block_count = mask_occ.shape[0]
    block_size = ao_count // block_count
    ri_blocks = mask_three.shape[0]
    first_row = dev_index * local_rows
    occ_local = green_occ * expand_rows(mask_occ, first_row, local_rows, block_size).astype(
        jnp.bfloat16
    )
    virt_local = green_virt * expand_rows(mask_virt, first_row, local_rows, block_size).astype(
        jnp.bfloat16
    )
    three_mask = lax.dynamic_slice_in_dim(
        jnp.repeat(mask_three, block_size, axis=1), first_row, local_rows, 1
    )
    masked = (
        three_centre.reshape(ri_blocks, block_size, local_rows, block_count, block_size)
        * three_mask[:, None, :, :, None].astype(jnp.bfloat16)
    ).reshape(ri_count, local_rows, ao_count)
    masked_rows = masked.reshape(ri_count * local_rows, ao_count)
    occ_full, virt_full = (
        lax.all_gather(occ_local, ("row", "col"), axis=0, tiled=True),
        lax.all_gather(virt_local, ("row", "col"), axis=0, tiled=True),
    )
    first_sum = jnp.dot(masked_rows, occ_full, preferred_element_type=jnp.float32)
    transformed = first_sum.astype(jnp.bfloat16).reshape(ri_count, local_rows, ao_count)
    arrived = lax.all_to_all(transformed, ("row", "col"), split_axis=2, concat_axis=1, tiled=True)
    swapped = jnp.swapaxes(arrived, 1, 2)
    swapped_rows = swapped.reshape(ri_count * local_rows, ao_count)
    second_sum = jnp.dot(swapped_rows, virt_full, preferred_element_type=jnp.float32)
    xform = second_sum.astype(jnp.bfloat16).reshape(ri_count, local_rows * ao_count)
    partial_value = lax.dot_general(
        xform,
        masked.reshape(ri_count, local_rows * ao_count),
        (((1,), (1,)), ((), ())),
        preferred_element_type=jnp.float32,
    )
    summed = lax.psum(partial_value, ("row", "col"))
    response = -summed / ao_count
    return (swapped, response)


def first_kernel(weight_ref, rows_ref, sent_ref):
    step, rows, depth = rows_ref.shape
    flat = rows_ref[...].reshape(step * rows, depth)
    product = lax.dot_general(
        weight_ref[...], flat, (((1,), (1,)), ((), ())), preferred_element_type=jnp.float32
    ).astype(jnp.bfloat16)
    owners, pairs, width, lanes = sent_ref.shape
    for pair in range(pairs):
        sent_ref[:, pair] = product[:, pair * lanes : (pair + 1) * lanes].reshape(
            owners, width, lanes
        )


def second_kernel(came_ref, weight_ref, *refs):
    half_ref, xform_ref = refs[-2:]
    owners, pairs, width, lanes = came_ref.shape
    for pair in range(pairs):
        for tile in range(owners // 2):
            even, odd = came_ref[2 * tile, pair], came_ref[2 * tile + 1, pair]
            spot = slice(tile * lanes, (tile + 1) * lanes)
            half_ref[2 * pair, :, spot] = jnp.concatenate(
                [even[:, :width], odd[:, :width]], axis=-1
            )
            half_ref[2 * pair + 1, :, spot] = jnp.concatenate(
                [even[:, width:], odd[:, width:]], axis=-1
            )
    step, rows, depth = half_ref.shape
    product = jnp.dot(
        half_ref[...].reshape(step * rows, depth),
        weight_ref[...],
        preferred_element_type=jnp.float32,
    )
    xform_ref[...] = product.astype(jnp.bfloat16).reshape(step, rows, depth)


def transform_chunk(weight, three_centre, first, chunk_size, owners):
    ri_count, rows, depth = three_centre.shape
    steps, offset = chunk_size // STEP, first // STEP
    return pl.pallas_call(
        first_kernel,
        grid=(steps,),
        in_specs=[
            pl.BlockSpec((depth, depth), lambda i: (0, 0)),
            pl.BlockSpec((STEP, rows, depth), lambda i: (offset + i, 0, 0)),
        ],
        out_specs=pl.BlockSpec((owners, STEP // 2, rows, 2 * rows), lambda i: (0, i, 0, 0)),
        out_shape=jax.ShapeDtypeStruct((owners, chunk_size // 2, rows, 2 * rows), jnp.bfloat16),
        compiler_params=pltpu.CompilerParams(vmem_limit_bytes=VMEM),
        cost_estimate=pl.CostEstimate(
            flops=2 * chunk_size * rows * depth * depth,
            bytes_accessed=4 * chunk_size * rows * depth + 2 * depth * depth,
            transcendentals=0,
        ),
    )(weight, three_centre)


def finish_chunk(came, weight, half, first, chunk_size, ri_count):
    owners, pairs, rows, lanes = came.shape
    depth = weight.shape[0]
    steps, offset = chunk_size // STEP, first // STEP
    operands = [came, weight]
    in_specs = [
        pl.BlockSpec((owners, STEP // 2, rows, lanes), lambda i: (0, i, 0, 0)),
        pl.BlockSpec((depth, depth), lambda i: (0, 0)),
    ]
    aliases = {}
    if half is not None:
        operands.append(half)
        in_specs.append(pl.BlockSpec(memory_space=pl.ANY))
        aliases = {2: 0}
    return pl.pallas_call(
        second_kernel,
        grid=(steps,),
        in_specs=in_specs,
        out_specs=[
            pl.BlockSpec((STEP, rows, depth), lambda i: (offset + i, 0, 0)),
            pl.BlockSpec((STEP, rows, depth), lambda i: (i, 0, 0)),
        ],
        out_shape=[
            jax.ShapeDtypeStruct((ri_count, rows, depth), jnp.bfloat16),
            jax.ShapeDtypeStruct((chunk_size, rows, depth), jnp.bfloat16),
        ],
        input_output_aliases=aliases,
        compiler_params=pltpu.CompilerParams(vmem_limit_bytes=VMEM),
        cost_estimate=pl.CostEstimate(
            flops=2 * chunk_size * rows * depth * depth,
            bytes_accessed=6 * chunk_size * rows * depth + 2 * depth * depth,
            transcendentals=0,
        ),
    )(*operands)


def spread(mask, block_size):
    return jnp.repeat(jnp.repeat(mask, block_size, 0), block_size, 1).astype(jnp.bfloat16)


def sum_over_devices(value, owners):
    pieces = value.reshape(owners, value.shape[0] // owners, value.shape[1])
    pieces = lax.all_to_all(pieces, AXES, split_axis=0, concat_axis=0, tiled=True)
    total = jnp.sum(pieces, axis=0)
    copies = jnp.broadcast_to(total[None], pieces.shape)
    copies = lax.all_to_all(copies, AXES, split_axis=0, concat_axis=0, tiled=True)
    return copies.reshape(value.shape)


def local_fused(owners, three_centre, green_occ, green_virt, mask_three, mask_occ, mask_virt):
    ri_count, rows, depth = three_centre.shape
    block_size = depth // mask_occ.shape[0]
    sizes = [ri_count // sum(SHARES) * share for share in SHARES]
    firsts = [sum(sizes[:chunk]) for chunk in range(len(sizes))]
    own_block = lax.axis_index(AXES) * rows // block_size
    own_mask = lax.dynamic_slice_in_dim(mask_three[0], own_block, 1, 0)
    both = jnp.concatenate([green_occ, green_virt], axis=1)
    both = lax.all_gather(both, AXES, axis=0, tiled=True)
    occ_full, virt_full = both[:, :depth], both[:, depth:]
    occ_weight = occ_full.T * spread(mask_occ.T * own_mask, block_size)
    virt_weight = virt_full * spread(mask_virt * own_mask, block_size)
    three_flat = lax.optimization_barrier(three_centre.reshape(ri_count, rows * depth))
    half, parts = None, []
    came = {}

    def send(chunk):
        block = transform_chunk(occ_weight, three_centre, firsts[chunk], sizes[chunk], owners)
        if chunk >= 2:
            block, came[chunk - 1], parts[chunk - 2] = lax.optimization_barrier(
                (block, came[chunk - 1], parts[chunk - 2])
            )
        elif chunk == 1:
            block, came[0] = lax.optimization_barrier((block, came[0]))
        came[chunk] = lax.all_to_all(block, AXES, split_axis=0, concat_axis=0, tiled=True)

    send(0)
    for chunk in range(len(sizes)):
        if chunk + 1 < len(sizes):
            send(chunk + 1)
        half, xform = finish_chunk(
            came[chunk], virt_weight, half, firsts[chunk], sizes[chunk], ri_count
        )
        flat = lax.optimization_barrier(xform.reshape(sizes[chunk], rows * depth))
        parts.append(
            lax.dot_general(
                flat, three_flat, (((1,), (1,)), ((), ())), preferred_element_type=jnp.float32
            )
        )
    response = -sum_over_devices(jnp.concatenate(parts, axis=0), owners) / depth
    return half, response


def local(owners, three_centre, green_occ, green_virt, mask_three, mask_occ, mask_virt):
    ri_count, rows, depth = three_centre.shape
    block_size = depth // mask_occ.shape[0]
    fits = (
        mask_three.shape[0] == 1
        and 2 * rows == 128
        and block_size % rows == 0
        and owners % 2 == 0
        and owners * rows == depth
        and ri_count % (sum(SHARES) * STEP) == 0
        and ri_count % owners == 0
    )
    body = functools.partial(local_fused, owners) if fits else local_plain
    return body(three_centre, green_occ, green_virt, mask_three, mask_occ, mask_virt)


def solution(mesh):
    owners = mesh.shape["row"] * mesh.shape["col"]
    in_specs = (
        P(None, ("row", "col"), None),
        P(("grp", "row", "col"), None),
        P(("grp", "row", "col"), None),
        P(),
        P("grp", None),
        P("grp", None),
    )
    out_specs = (P("grp", ("row", "col"), None), P("grp", None))
    return jax.shard_map(
        functools.partial(local, owners), mesh=mesh, in_specs=in_specs, out_specs=out_specs, check_vma=False)
```
